1024 devices in a mesh: band: 16 (over x, core), dom: 64 (over z, y).
Axes of the slice: x: 8, y: 8, z: 8, core: 2. Of those that a mesh axis runs over, the one named last changes fastest.
Arguments:
- grid_latent: bfloat16 [262144, 512], P(('band', 'dom')), may hold values from -6 to 6
- mesh_latent: bfloat16 [32768, 512], P(('band', 'dom')), may hold values from -6 to 6
- send_rows: int32 [65536, 16], P(('band', 'dom')), may hold values from 0 to 255, as said below
- send_count: int32 [65536], P(('band', 'dom')), may hold values from 1 to 16, as said below
- enc_sender: int32 [524288], P(('band', 'dom')), may hold values from 0 to 1023, as said below
- enc_receiver: int32 [524288], P(('band', 'dom')), may hold values from 0 to 31, as said below
- move_to: int32 [32768], P(('band', 'dom')), may hold values from 0 to 511, as said below
- proc_sender: int32 [524288], P(('band', 'dom')), may hold values from 0 to 31
- proc_receiver: int32 [524288], P(('band', 'dom')), may hold values from 0 to 31
- enc_edge_w1: bfloat16 [1024, 512], replicated, may hold values from -0.1875 to 0.1875
- enc_edge_b1: float32 [512], replicated, may hold values from -3 to 3
- enc_edge_w2: bfloat16 [512, 512], replicated, may hold values from -0.25 to 0.25
- enc_edge_b2: float32 [512], replicated, may hold values from -2 to 2
- enc_node_w1: bfloat16 [1024, 512], replicated, may hold values from -0.1875 to 0.1875
- enc_node_b1: float32 [512], replicated, may hold values from -3 to 3
- enc_node_w2: bfloat16 [512, 512], replicated, may hold values from -0.25 to 0.25
- enc_node_b2: float32 [512], replicated, may hold values from -3 to 3
- enc_gain: float32 [512], replicated, may hold values from 0.1 to 1.9
- proc_edge_w1: bfloat16 [1024, 512], replicated, may hold values from -0.1875 to 0.1875
- proc_edge_b1: float32 [512], replicated, may hold values from -3 to 3
- proc_edge_w2: bfloat16 [512, 512], replicated, may hold values from -0.25 to 0.25
- proc_edge_b2: float32 [512], replicated, may hold values from -2 to 2
- proc_node_w1: bfloat16 [1024, 512], replicated, may hold values from -0.1875 to 0.1875
- proc_node_b1: float32 [512], replicated, may hold values from -3 to 3
- proc_node_w2: bfloat16 [512, 512], replicated, may hold values from -0.25 to 0.25
- proc_node_b2: float32 [512], replicated, may hold values from -3 to 3
- proc_gain: float32 [512], replicated, may hold values from 0.1 to 1.9
Outputs:
- mesh_out: bfloat16 [32768, 512], P(('band', 'dom'))
The draws below stay inside these ranges and needn't reach their ends.
Inputs may be any that keep to these rules, and one draw needn't show every extreme that they name: `send_rows`: entries of a sender's list at or past the matching send_count are unused. `send_count`: in every band group one receiving dom index gets 16 rows from every sender. `enc_sender`: each value is s * 16 + k for a sender dom index s and k below the count that s sends to this device. `enc_receiver`: Non-decreasing within each device's 512 edges. `move_to`: value c * 32 + r: the row goes to row r of the device with band index c and the same dom index; a device sends at most 8 rows to other band indices, exactly 8 for some device; within each dom index the values form a permutation.
All inputs are finite; a program needn't handle non-finite values.
Results may differ from the reference program's by a relative error of at most 0.01.
Values may be sent and summed in bfloat16 or wider, within the bound.
A program may use at most 32 MiB of HBM per device.

```python
import jax
import jax.numpy as jnp
from jax import lax

D = 512
H = 512
G_DEV = 256
M_DEV = 32
CAP = 16
E_DEV = 512
PE_DEV = 512
MOVE_CAP = 8
GRID = 262144
MESH = 32768
N_BAND = 16
N_DOM = 64
DEVICES = 1024


def grid_plan(key):
    keys = jax.random.split(jax.random.fold_in(key, 101), 7)
    ceiling = jax.random.randint(keys[0], (N_BAND, N_DOM), max(1, CAP // 4), CAP + 1)
    full_target = jax.random.randint(keys[1], (N_BAND,), 0, N_DOM)
    is_full = jnp.arange(N_DOM)[None, :] == full_target[:, None]
    ceiling = jnp.where(is_full, CAP, ceiling)
    counts = jax.random.randint(keys[2], (N_BAND, N_DOM, N_DOM), 1, ceiling[:, None, :] + 1)
    counts = jnp.where(is_full[:, None, :], CAP, counts)
    rows = jax.random.randint(keys[3], (N_BAND, N_DOM, N_DOM, CAP), 0, G_DEV)
    source = jax.random.randint(keys[4], (N_BAND, N_DOM, E_DEV), 0, N_DOM)
    incoming = jnp.transpose(counts, (0, 2, 1))
    limit = jnp.take_along_axis(incoming, source, axis=2)
    offset = jax.random.randint(keys[5], (N_BAND, N_DOM, E_DEV), 0, limit)
    slots = source * CAP + offset
    targets = jnp.sort(jax.random.randint(keys[6], (N_BAND, N_DOM, E_DEV), 0, M_DEV), axis=-1)
    return (rows, counts, slots, targets)


def relay_group(key):
    keys = jax.random.split(key, 2)
    perms = jax.vmap(lambda sub: jax.random.permutation(sub, M_DEV))(jax.random.split(keys[0], N_BAND))
    offsets = jax.random.randint(keys[1], (MOVE_CAP,), 1, N_BAND)
    offsets = jnp.where(jnp.arange(MOVE_CAP) == 0, N_BAND // 2, offsets)
    offsets = jnp.concatenate([offsets, jnp.zeros((M_DEV - MOVE_CAP,), jnp.int32)])
    bands = jnp.arange(N_BAND, dtype=jnp.int32)[:, None]
    rank = jnp.arange(M_DEV, dtype=jnp.int32)[None, :]
    dest_band = (bands + offsets[None, :]) % N_BAND
    dest_slot = perms[dest_band, jnp.broadcast_to(rank, (N_BAND, M_DEV))]
    value = dest_band * M_DEV + dest_slot
    return jnp.zeros((N_BAND, M_DEV), jnp.int32).at[jnp.broadcast_to(bands, (N_BAND, M_DEV)), perms].set(value)


def relay_plan(key):
    forward = jax.vmap(relay_group)(jax.random.split(jax.random.fold_in(key, 202), N_DOM))
    return jnp.transpose(forward, (1, 0, 2)).reshape(-1)


def draw_send_rows(key, part):
    rows, counts, slots, targets = grid_plan(key)
    return rows.reshape(DEVICES * N_DOM, CAP).astype(jnp.int32)


def draw_send_count(key, part):
    rows, counts, slots, targets = grid_plan(key)
    return counts.reshape(DEVICES * N_DOM).astype(jnp.int32)


def draw_enc_sender(key, part):
    rows, counts, slots, targets = grid_plan(key)
    return slots.reshape(DEVICES * E_DEV).astype(jnp.int32)


def draw_enc_receiver(key, part):
    rows, counts, slots, targets = grid_plan(key)
    return targets.reshape(DEVICES * E_DEV).astype(jnp.int32)


def draw_move_to(key, part):
    forward = relay_plan(key)
    return forward.astype(jnp.int32)


def with_ends(array, key, low, top_value):
    extent = array.shape
    index_at = [jax.random.randint(jax.random.fold_in(key, axis), (), 0, extent[axis]) for axis in range(len(extent))]
    array = array.at[tuple(index_at)].set(low)
    longest = extent.index(max(extent))
    index_at[longest] = (index_at[longest] + 1) % extent[longest]
    return array.at[tuple(index_at)].set(top_value)


def shard_levels(own_key, shape, pieces, smallest, top_value):
    factor_of = 1.0
    for axis_at, shards_of in pieces:
        draws = jax.random.uniform(jax.random.fold_in(jax.random.fold_in(own_key, 6), axis_at), (shards_of,), jnp.float32, smallest / len(pieces), top_value / len(pieces))
        factor_of = factor_of * jnp.repeat(jnp.exp(draws), shape[axis_at] // shards_of).reshape((-1,) + (1,) * (len(shape) - 1 - axis_at))
    return factor_of


def gaussian(own_key, dims, scale, most, cuts=(), kind=jnp.bfloat16):
    loudness = shard_levels(own_key, dims, cuts, -0.22, 0.18) if cuts else 1.0
    result = jax.random.normal(own_key, dims, jnp.float32) * scale * loudness
    return jnp.minimum(jnp.maximum(result, -most), most).astype(kind)


def setup_inputs(seed: int = 0) -> dict:
    splits = jax.random.split(jax.random.key(seed), 28)
    return {
        "grid_latent": gaussian(splits[0], (GRID, D), 1.0, 6.0, ((0, 1024),)),
        "mesh_latent": gaussian(splits[1], (MESH, D), 1.0, 6.0, ((0, 1024),)),
        "send_rows": draw_send_rows(jax.random.fold_in(splits[27], 71), 0),
        "send_count": draw_send_count(jax.random.fold_in(splits[27], 71), 0),
        "enc_sender": draw_enc_sender(jax.random.fold_in(splits[27], 71), 0),
        "enc_receiver": draw_enc_receiver(jax.random.fold_in(splits[27], 71), 0),
        "move_to": draw_move_to(jax.random.fold_in(splits[27], 71), 0),
        "proc_sender": with_ends(jax.random.randint(splits[7], (DEVICES * PE_DEV,), 0, M_DEV), jax.random.fold_in(splits[7], 1), 0, M_DEV - 1).astype(jnp.int32),
        "proc_receiver": with_ends(jax.random.randint(splits[8], (DEVICES * PE_DEV,), 0, M_DEV), jax.random.fold_in(splits[8], 1), 0, M_DEV - 1).astype(jnp.int32),
        "enc_edge_w1": gaussian(splits[9], (2 * D, H), (2 * D) ** -0.5, 0.1875),
        "enc_edge_b1": gaussian(splits[10], (H,), 0.5, 3.0, (), jnp.float32),
        "enc_edge_w2": gaussian(splits[11], (H, D), H ** -0.5, 0.25),
        "enc_edge_b2": gaussian(splits[12], (D,), 0.3, 2.0, (), jnp.float32),
        "enc_node_w1": gaussian(splits[13], (2 * D, H), (2 * D) ** -0.5, 0.1875),
        "enc_node_b1": gaussian(splits[14], (H,), 0.5, 3.0, (), jnp.float32),
        "enc_node_w2": gaussian(splits[15], (H, D), H ** -0.5, 0.25),
        "enc_node_b2": gaussian(splits[16], (D,), 0.5, 3.0, (), jnp.float32),
        "enc_gain": jnp.clip(1.0 + 0.18 * jax.random.normal(splits[17], (D,), jnp.float32), 0.1, 1.9),
        "proc_edge_w1": gaussian(splits[18], (2 * D, H), (2 * D) ** -0.5, 0.1875),
        "proc_edge_b1": gaussian(splits[19], (H,), 0.5, 3.0, (), jnp.float32),
        "proc_edge_w2": gaussian(splits[20], (H, D), H ** -0.5, 0.25),
        "proc_edge_b2": gaussian(splits[21], (D,), 0.3, 2.0, (), jnp.float32),
        "proc_node_w1": gaussian(splits[22], (2 * D, H), (2 * D) ** -0.5, 0.1875),
        "proc_node_b1": gaussian(splits[23], (H,), 0.5, 3.0, (), jnp.float32),
        "proc_node_w2": gaussian(splits[24], (H, D), H ** -0.5, 0.25),
        "proc_node_b2": gaussian(splits[25], (D,), 0.5, 3.0, (), jnp.float32),
        "proc_gain": jnp.clip(1.0 + 0.18 * jax.random.normal(splits[26], (D,), jnp.float32), 0.1, 1.9),
    }


def node_update(mesh, agg, node_w1, node_b1, node_w2, node_b2, gain):
    width = mesh.shape[1]
    agg_round = agg.astype(jnp.bfloat16)
    pre = jnp.dot(mesh, node_w1[:width], preferred_element_type=jnp.float32)
    pre = pre + jnp.dot(agg_round, node_w1[width:], preferred_element_type=jnp.float32) + node_b1
    hidden = jax.nn.silu(pre).astype(jnp.bfloat16)
    update = jnp.dot(hidden, node_w2, preferred_element_type=jnp.float32) + node_b2
    center = update - lax.optimization_barrier(jnp.mean(update, axis=-1, keepdims=True))
    spread = lax.optimization_barrier(jnp.mean(center * center, axis=-1, keepdims=True))
    normed = center * lax.rsqrt(spread + 1e-05)
    return (mesh.astype(jnp.float32) + gain * normed).astype(jnp.bfloat16)

def edge_sum(send_proj, recv_proj, sender, receiver, bias_one, weight_two, bias_two, count_rows):
    pre = send_proj[sender] + recv_proj[receiver] + bias_one
    hidden = jax.nn.silu(pre).astype(jnp.bfloat16)
    message = (jnp.dot(hidden, weight_two, preferred_element_type=jnp.float32) + bias_two).astype(jnp.bfloat16)
    return jax.ops.segment_sum(message.astype(jnp.float32), receiver, num_segments=count_rows)

def reference(grid_latent, mesh_latent, send_rows, send_count, enc_sender, enc_receiver, move_to, proc_sender, proc_receiver, enc_edge_w1, enc_edge_b1, enc_edge_w2, enc_edge_b2, enc_node_w1, enc_node_b1, enc_node_w2, enc_node_b2, enc_gain, proc_edge_w1, proc_edge_b1, proc_edge_w2, proc_edge_b2, proc_node_w1, proc_node_b1, proc_node_w2, proc_node_b2, proc_gain):
    grid_blocks = grid_latent.reshape(N_BAND, N_DOM, G_DEV, D)
    row_lists = send_rows.reshape(N_BAND, N_DOM, N_DOM, CAP)
    row_counts = send_count.reshape(N_BAND, N_DOM, N_DOM)
    mesh_blocks = mesh_latent.reshape(DEVICES, M_DEV, D)
    senders = enc_sender.reshape(DEVICES, E_DEV)
    receivers = enc_receiver.reshape(DEVICES, E_DEV)

    def encode(index):
        band_at = index // N_DOM
        dom_at = index % N_DOM
        chosen = row_lists[band_at][:, dom_at, :]
        counts = row_counts[band_at][:, dom_at]
        picked = grid_blocks[band_at][jnp.arange(N_DOM)[:, None], chosen]
        keep = jnp.arange(CAP)[None, :] < counts[:, None]
        picked = jnp.where(keep[:, :, None], picked, jnp.zeros_like(picked))
        send_proj = jnp.dot(picked.reshape(N_DOM * CAP, D), enc_edge_w1[:D], preferred_element_type=jnp.float32)
        mesh = mesh_blocks[index]
        recv_proj = jnp.dot(mesh, enc_edge_w1[D:], preferred_element_type=jnp.float32)
        agg = edge_sum(send_proj, recv_proj, senders[index], receivers[index], enc_edge_b1, enc_edge_w2, enc_edge_b2, M_DEV)
        return node_update(mesh, agg, enc_node_w1, enc_node_b1, enc_node_w2, enc_node_b2, enc_gain)
    mesh_enc = lax.map(encode, jnp.arange(DEVICES, dtype=jnp.int32))
    enc_grid = mesh_enc.reshape(N_BAND, N_DOM, M_DEV, D)
    source = jnp.transpose(enc_grid, (1, 0, 2, 3)).reshape(N_DOM, N_BAND * M_DEV, D)
    target = jnp.transpose(move_to.reshape(N_BAND, N_DOM, M_DEV), (1, 0, 2)).reshape(N_DOM, N_BAND * M_DEV)
    doms = jnp.arange(N_DOM, dtype=jnp.int32)[:, None]
    placed = jnp.zeros((N_DOM, N_BAND * M_DEV, D), jnp.bfloat16).at[doms, target].set(source)
    proc_grid = placed.reshape(N_DOM, N_BAND, M_DEV, D)
    psend = proc_sender.reshape(DEVICES, PE_DEV)
    precv = proc_receiver.reshape(DEVICES, PE_DEV)

    def process(index):
        band_at = index // N_DOM
        dom_at = index % N_DOM
        proc_in = proc_grid[dom_at, band_at]
        send_proj = jnp.dot(proc_in, proc_edge_w1[:D], preferred_element_type=jnp.float32)
        recv_proj = jnp.dot(proc_in, proc_edge_w1[D:], preferred_element_type=jnp.float32)
        agg = edge_sum(send_proj, recv_proj, psend[index], precv[index], proc_edge_b1, proc_edge_w2, proc_edge_b2, M_DEV)
        return node_update(proc_in, agg, proc_node_w1, proc_node_b1, proc_node_w2, proc_node_b2, proc_gain)
    mesh_out = lax.map(process, jnp.arange(DEVICES, dtype=jnp.int32))
    return mesh_out.reshape(MESH, D)
```

```python
import functools

import jax
import jax.numpy as jnp
import numpy as np
from jax import lax
from jax.experimental import pallas as pl
from jax.experimental.pallas import tpu as pltpu
from jax.sharding import PartitionSpec as P

MESH = pl.DeviceIdType.MESH
F32 = jnp.float32
BF16 = jnp.bfloat16
I32 = jnp.int32
CAP = 16
MOVE = 8
WEIGHTS = 8


def iota(shape, dim):
    return lax.broadcasted_iota(I32, shape, dim)


def dot(a, b):
    return jnp.dot(a, b, preferred_element_type=F32)


def one_hot(mask):
    return jnp.where(mask, 1.0, 0.0).astype(BF16)


def silu(v):
    return v / (1.0 + jnp.exp(-v))


def halves(v):
    high = v.astype(BF16)
    return jnp.concatenate([high, (v - high.astype(F32)).astype(BF16)], axis=0)


def node_out(rows, pre, agg, w1, w2, b2, gain):
    width = rows.shape[1]
    z = silu(pre + dot(agg, w1[width:])).astype(BF16)
    u = dot(z, w2[...]) + b2
    center = u - jnp.mean(u, axis=-1, keepdims=True)
    spread = jnp.mean(center * center, axis=-1, keepdims=True)
    return (rows.astype(F32) + gain * (center * lax.rsqrt(spread + 1e-05))).astype(BF16)


def aggregate(hidden, hot_t, w2, b2):
    rows = hot_t.shape[0]
    two = dot(halves(dot(hot_t, hidden)), w2[...])
    count = jnp.sum(hot_t.astype(F32), axis=1, keepdims=True)
    return (two[:rows] + two[rows:] + count * b2).astype(BF16)


def lanes_to_rows(row):
    return jnp.broadcast_to(row, (128, row.shape[1])).T


def kernel(
    bands, zs, ys, order,
    grid, rows, send_rows, send_count, enc_s, enc_r, move_to, proc_s, proc_r,
    e_b1, e_b2, en_b1, en_b2, e_gain, p_b1, p_b2, pn_b1, pn_b2, p_gain,
    *rest,
):
    hbm, out = rest[:WEIGHTS], rest[WEIGHTS]
    held = rest[WEIGHTS + 1 : 2 * WEIGHTS + 1]
    (send, recv, pick, base, total, meta_out, meta_in, move_out, move_in,
     w_sem, ss, rs, ms, mr, vs, vr) = rest[2 * WEIGHTS + 1 :]
    e_w1, e_w2, n_w1, n_w2, p_w1, p_w2, q_w1, q_w2 = held
    doms = zs * ys
    width = grid.shape[1]
    count = rows.shape[0]
    edges = enc_s.shape[1]
    slots = doms * CAP
    chunks = rs.shape[0]
    per = doms // chunks
    band, dom = lax.axis_index("band"), lax.axis_index("dom")
    z, y = dom // ys, dom % ys

    barrier = pltpu.get_barrier_semaphore()
    for a, c in order:
        there = ((z + a) % zs) * ys + (y + c) % ys
        pl.semaphore_signal(barrier, inc=1, device_id=(band, there), device_id_type=MESH)
    for k in range(1, bands):
        pl.semaphore_signal(barrier, inc=1, device_id=((band + k) % bands, dom), device_id_type=MESH)

    loads = [pltpu.make_async_copy(hbm[i], held[i], w_sem.at[i]) for i in range(WEIGHTS)]
    for load in loads:
        load.start()

    block = min(256, slots)
    listed = send_rows[...].astype(F32).astype(BF16)
    counts = send_count[...].astype(F32)

    def gather(i, carry):
        slot = iota((block, doms), 0) + i * block
        rel = slot // CAP
        there = ((z + rel // ys) % zs) * ys + (y + rel % ys) % ys
        peer = there == iota((block, doms), 1)
        mine = dot(one_hot(peer), listed)
        lane = (iota((block, CAP), 0) % CAP) == iota((block, CAP), 1)
        index = dot(jnp.where(lane, mine, 0.0).astype(BF16), jnp.ones((CAP, grid.shape[0]), BF16))
        limit = dot(jnp.where(peer, counts, 0.0).astype(BF16), jnp.ones((doms, grid.shape[0]), BF16))
        at = iota((block, grid.shape[0]), 0) % CAP
        hot = (index == iota((block, grid.shape[0]), 1).astype(F32)) & (at.astype(F32) < limit)
        send[pl.ds(pl.multiple_of(i * block, block), block), :] = dot(one_hot(hot), grid[...]).astype(BF16)
        return carry

    lax.fori_loop(0, slots // block, gather, 0)

    dest = move_to[...]
    leaves = (dest // count) != band
    before = one_hot(iota((count, count), 0) < iota((count, count), 1))
    rank = dot(jnp.broadcast_to(one_hot(leaves), (8, count)), before)[:MOVE]
    packs = (rank == iota((MOVE, count), 0).astype(F32)) & leaves
    goes = jnp.sum(jnp.where(packs, (dest + 1).astype(F32), 0.0), axis=1, keepdims=True) - 1.0
    goes = jnp.broadcast_to(goes, (MOVE, 128)).astype(I32)
    meta_out[...] = jnp.concatenate([goes, goes], axis=0)
    meta_in[0] = jnp.full((2 * MOVE, 128), -1, I32)
    move_in[0] = jnp.zeros((2 * MOVE, width // 2), BF16)

    pl.semaphore_wait(barrier, len(order) + bands - 1)

    for a, c in order:
        there = ((z + a) % zs) * ys + (y + c) % ys
        at = (a * ys + c) * CAP
        pltpu.make_async_remote_copy(
            send.at[pl.ds(at, CAP)], recv.at[pl.ds(at, CAP)], ss.at[0], rs.at[(a * ys + c) // per],
            device_id=(band, there), device_id_type=MESH,
        ).start()
    for k in range(1, bands):
        pltpu.make_async_remote_copy(
            meta_out, meta_in.at[k], ms.at[0], mr.at[0],
            device_id=((band + k) % bands, dom), device_id_type=MESH,
        ).start()
    recv[pl.ds(0, CAP), :] = send[pl.ds(0, CAP), :]

    sender = enc_s[...]
    from_dom = sender // CAP
    rel_z = (z - from_dom // ys + zs) % zs
    rel_y = (y - from_dom % ys + ys) % ys
    place = lanes_to_rows((rel_z * ys + rel_y) * CAP + sender % CAP)
    for i in range(slots // 128):
        pick[:, pl.ds(i * 128, 128)] = one_hot(place == iota((edges, 128), 1) + i * 128)
    lane = iota((edges, 128), 1)
    receiver = lanes_to_rows(enc_r[...])
    recv_hot = one_hot(((lane % count) == receiver) & (lane < 2 * count))
    hot_t = one_hot(iota((count, edges), 0) == enc_r[...])
    loads[0].wait()
    recv_proj = dot(rows[...], e_w1[width:]) + e_b1[...]
    stack = jnp.concatenate([halves(recv_proj), jnp.zeros((128 - 2 * count, recv_proj.shape[1]), BF16)], axis=0)
    base[...] = dot(recv_hot, stack)
    loads[2].wait()
    node_pre = dot(rows[...], n_w1[:width]) + en_b1[...]
    proc_send, proc_recv = lanes_to_rows(proc_s[...]), lanes_to_rows(proc_r[...])
    proc_hot = one_hot((lane % count) == jnp.where((lane // count) % 2 == 0, proc_send, proc_recv))
    proc_hot_t = one_hot(iota((count, edges), 0) == proc_r[...])
    pack = one_hot(packs)
    stays = one_hot(dest - band * count == iota((count, count), 0))
    pltpu.make_async_remote_copy(
        meta_in.at[pl.ds(1, bands - 1)], meta_in.at[pl.ds(1, bands - 1)], ms.at[0], mr.at[0],
        device_id=((band + 1) % bands, dom), device_id_type=MESH,
    ).wait()
    moved = meta_in[...].reshape(bands * 2 * MOVE, 128)
    moved = jnp.concatenate([moved[i * 128 : (i + 1) * 128].T for i in range(bands * 2 * MOVE // 128)], axis=1)
    lands = moved[:count] == iota((count, bands * 2 * MOVE), 0) + band * count
    left = (iota((count, bands * 2 * MOVE), 1) % (2 * MOVE)) < MOVE
    place_in = jnp.concatenate([one_hot(lands & left), one_hot(lands & jnp.logical_not(left))], axis=0)
    for i in (1, 3, 4, 5, 6, 7):
        loads[i].wait()

    span = per * CAP
    for i in range(chunks):
        first = 1 if i == 0 else i * per
        blocks = per - 1 if i == 0 else per
        landed = recv.at[pl.ds(first * CAP, blocks * CAP)]
        pltpu.make_async_remote_copy(
            landed, landed, ss.at[0], rs.at[i], device_id=(band, (z * ys + (y + 1) % ys)), device_id_type=MESH
        ).wait_recv()
        part = dot(pick[:, pl.ds(i * span, span)], recv[pl.ds(i * span, span), :])
        if i == 0:
            total[...] = part
        elif i < chunks - 1:
            total[...] += part
    gathered = (total[...] + part).astype(BF16) if chunks > 1 else part.astype(BF16)
    hidden = silu(base[...] + dot(gathered, e_w1[:width])).astype(BF16)
    agg = aggregate(hidden, hot_t, e_w2, e_b2[...])
    mesh_enc = node_out(rows[...], node_pre, agg, n_w1, n_w2, en_b2[...], e_gain[...])

    packed = dot(pack, mesh_enc)
    move_out[...] = jnp.concatenate([packed[:, : width // 2], packed[:, width // 2 :]], axis=0).astype(BF16)
    for k in range(1, bands):
        pltpu.make_async_remote_copy(
            move_out, move_in.at[k], vs.at[0], vr.at[0],
            device_id=((band + k) % bands, dom), device_id_type=MESH,
        ).start()
    kept = dot(stays, mesh_enc)
    pltpu.make_async_remote_copy(
        move_in.at[pl.ds(1, bands - 1)], move_in.at[pl.ds(1, bands - 1)], vs.at[0], vr.at[0],
        device_id=((band + 1) % bands, dom), device_id_type=MESH,
    ).wait()
    came = dot(place_in, move_in[...].reshape(bands * 2 * MOVE, width // 2))
    proc_in = (kept + jnp.concatenate([came[:count], came[count:]], axis=1)).astype(BF16)

    projected = jnp.concatenate([dot(proc_in, p_w1[:width]), dot(proc_in, p_w1[width:]) + p_b1[...]], axis=0)
    hidden = silu(dot(proc_hot, halves(projected))).astype(BF16)
    node_pre = dot(proc_in, q_w1[:width]) + pn_b1[...]
    agg = aggregate(hidden, proc_hot_t, p_w2, p_b2[...])
    out[...] = node_out(proc_in, node_pre, agg, q_w1, q_w2, pn_b2[...], p_gain[...])
    outgoing = send.at[pl.ds(CAP, slots - CAP)]
    pltpu.make_async_remote_copy(
        outgoing, outgoing, ss.at[0], rs.at[0], device_id=(band, (z * ys + (y + 1) % ys)), device_id_type=MESH
    ).wait_send()


def solution(mesh):
    bands, doms = mesh.shape["band"], mesh.shape["dom"]
    zs = 2 ** ((doms.bit_length() - 1) // 2)
    ys = doms // zs
    offsets = [(a, c) for a in range(zs) for c in range(ys) if (a, c) != (0, 0)]
    order = [offsets[i] for i in np.random.RandomState(0).permutation(len(offsets))]

    def shards(
        grid_latent, mesh_latent, send_rows, send_count, enc_sender, enc_receiver, move_to, proc_sender, proc_receiver,
        enc_edge_w1, enc_edge_b1, enc_edge_w2, enc_edge_b2, enc_node_w1, enc_node_b1, enc_node_w2, enc_node_b2, enc_gain,
        proc_edge_w1, proc_edge_b1, proc_edge_w2, proc_edge_b2, proc_node_w1, proc_node_b1, proc_node_w2, proc_node_b2, proc_gain,
    ):
        count, width = mesh_latent.shape
        edges = enc_sender.shape[0]
        slots = doms * CAP
        weights = (enc_edge_w1, enc_edge_w2, enc_node_w1, enc_node_w2, proc_edge_w1, proc_edge_w2, proc_node_w1, proc_node_w2)
        small = (send_count, enc_sender, enc_receiver, move_to, proc_sender, proc_receiver,
                 enc_edge_b1, enc_edge_b2, enc_node_b1, enc_node_b2, enc_gain,
                 proc_edge_b1, proc_edge_b2, proc_node_b1, proc_node_b2, proc_gain)
        small = [a.reshape(1, -1) for a in small]
        vmem = pl.BlockSpec(memory_space=pltpu.VMEM)
        dma = pltpu.SemaphoreType.DMA
        chunks = max(1, slots // 256)
        return pl.pallas_call(
            functools.partial(kernel, bands, zs, ys, order),
            out_shape=jax.ShapeDtypeStruct((count, width), BF16),
            in_specs=[vmem] * (3 + len(small)) + [pl.BlockSpec(memory_space=pl.ANY)] * WEIGHTS,
            out_specs=vmem,
            scratch_shapes=[pltpu.VMEM(w.shape, w.dtype) for w in weights] + [
                pltpu.VMEM((slots, width), BF16),
                pltpu.VMEM((slots, width), BF16),
                pltpu.VMEM((edges, slots), BF16),
                pltpu.VMEM((edges, enc_edge_w1.shape[1]), F32),
                pltpu.VMEM((edges, width), F32),
                pltpu.VMEM((2 * MOVE, 128), I32),
                pltpu.VMEM((bands, 2 * MOVE, 128), I32),
                pltpu.VMEM((2 * MOVE, width // 2), BF16),
                pltpu.VMEM((bands, 2 * MOVE, width // 2), BF16),
                dma((WEIGHTS,)), dma((1,)), dma((chunks,)), dma((1,)), dma((1,)), dma((1,)), dma((1,)),
            ],
            compiler_params=pltpu.CompilerParams(
                collective_id=0, has_side_effects=True, vmem_limit_bytes=40 * 1024 * 1024
            ),
            name="encode_process",
        )(grid_latent, mesh_latent, send_rows, *small, *weights)

    split, whole = P(("band", "dom")), P()
    return jax.shard_map(
        shards,
        mesh=mesh,
        in_specs=(P(("band", "dom"), None),) * 3 + (split,) * 6 + (whole,) * 18,
        out_specs=P(("band", "dom"), None),
        check_vma=False,
    )
```

```python
import functools

import jax
import jax.numpy as jnp
import numpy as np
from jax import lax
from jax.experimental import pallas as pl
from jax.experimental.pallas import tpu as pltpu
from jax.sharding import PartitionSpec as P

MESH = pl.DeviceIdType.MESH
F32 = jnp.float32
BF16 = jnp.bfloat16
I32 = jnp.int32
CAP = 16
MOVE = 8
ARGS = 27


def iota(shape, dim):
    return lax.broadcasted_iota(I32, shape, dim)


def dot(a, b):
    return jnp.dot(a, b, preferred_element_type=F32)


def one_hot(mask):
    return jnp.where(mask, 1.0, 0.0).astype(BF16)


def silu(v):
    return v / (1.0 + jnp.exp(-v))


def halves(v):
    high = v.astype(BF16)
    return jnp.concatenate([high, (v - high.astype(F32)).astype(BF16)], axis=0)


def node_out(rows, pre, agg, w1, w2, b2, gain):
    width = rows.shape[1]
    z = silu(pre + dot(agg, w1[width:])).astype(BF16)
    u = dot(z, w2[...]) + b2
    center = u - jnp.mean(u, axis=-1, keepdims=True)
    spread = jnp.mean(center * center, axis=-1, keepdims=True)
    return (rows.astype(F32) + gain * (center * lax.rsqrt(spread + 1e-05))).astype(BF16)


def aggregate(hidden, hot_t, w2, b2):
    rows = hot_t.shape[0]
    two = dot(halves(dot(hot_t, hidden)), w2[...])
    count = jnp.sum(hot_t.astype(F32), axis=1, keepdims=True)
    return (two[:rows] + two[rows:] + count * b2).astype(BF16)


def lanes_to_rows(row):
    return jnp.broadcast_to(row, (128, row.shape[1])).T


def kernel(
    bands, zs, ys, order,
    *refs,
):
    hbm, out = refs[:ARGS], refs[ARGS]
    held = refs[ARGS + 1 : 2 * ARGS + 1]
    (send, recv, pick, base, total, meta_out, meta_in, move_out, move_in,
     in_sem, ss, rs, ms, mr, vs, vr) = refs[2 * ARGS + 1 :]
    (send_rows, send_count, grid, move_to, enc_s, rows, enc_r, proc_s, proc_r,
     e_w1, e_b1, n_w1, en_b1, e_w2, e_b2, n_w2, en_b2, e_gain,
     p_w1, p_b1, p_w2, p_b2, q_w1, pn_b1, q_w2, pn_b2, p_gain) = held
    doms = zs * ys
    width = grid.shape[1]
    count = rows.shape[0]
    edges = enc_s.shape[1]
    slots = doms * CAP
    chunks = rs.shape[0]
    per = doms // chunks
    band, dom = lax.axis_index("band"), lax.axis_index("dom")
    z, y = dom // ys, dom % ys

    barrier = pltpu.get_barrier_semaphore()
    for a, c in order:
        there = ((z + a) % zs) * ys + (y + c) % ys
        pl.semaphore_signal(barrier, inc=1, device_id=(band, there), device_id_type=MESH)
    for k in range(1, bands):
        pl.semaphore_signal(barrier, inc=1, device_id=((band + k) % bands, dom), device_id_type=MESH)

    loads = [pltpu.make_async_copy(hbm[i], held[i], in_sem.at[i]) for i in range(ARGS)]
    for load in loads:
        load.start()
    for load in loads[:3]:
        load.wait()

    block = min(256, slots)
    listed = send_rows[...].astype(F32).astype(BF16)
    counts = send_count[...].astype(F32)

    def gather(i, carry):
        slot = iota((block, doms), 0) + i * block
        rel = slot // CAP
        there = ((z + rel // ys) % zs) * ys + (y + rel % ys) % ys
        peer = there == iota((block, doms), 1)
        mine = lax.dot_general(one_hot(peer), listed, (((1,), (1,)), ((), ())), preferred_element_type=F32)
        lane = (iota((block, CAP), 0) % CAP) == iota((block, CAP), 1)
        index = dot(jnp.where(lane, mine, 0.0).astype(BF16), jnp.ones((CAP, grid.shape[0]), BF16))
        limit = dot(jnp.where(peer, counts, 0.0).astype(BF16), jnp.ones((doms, grid.shape[0]), BF16))
        at = iota((block, grid.shape[0]), 0) % CAP
        hot = (index == iota((block, grid.shape[0]), 1).astype(F32)) & (at.astype(F32) < limit)
        send[pl.ds(pl.multiple_of(i * block, block), block), :] = dot(one_hot(hot), grid[...]).astype(BF16)
        return carry

    lax.fori_loop(0, slots // block, gather, 0)

    for load in loads[3:9]:
        load.wait()
    dest = move_to[...]
    leaves = (dest // count) != band
    before = one_hot(iota((count, count), 0) < iota((count, count), 1))
    rank = dot(jnp.broadcast_to(one_hot(leaves), (8, count)), before)[:MOVE]
    packs = (rank == iota((MOVE, count), 0).astype(F32)) & leaves
    goes = jnp.sum(jnp.where(packs, (dest + 1).astype(F32), 0.0), axis=1, keepdims=True) - 1.0
    goes = jnp.broadcast_to(goes, (MOVE, 128)).astype(I32)
    meta_out[...] = jnp.concatenate([goes, goes], axis=0)
    meta_in[0] = jnp.full((2 * MOVE, 128), -1, I32)
    move_in[0] = jnp.zeros((2 * MOVE, width // 2), BF16)

    pl.semaphore_wait(barrier, len(order) + bands - 1)

    for a, c in order:
        there = ((z + a) % zs) * ys + (y + c) % ys
        at = (a * ys + c) * CAP
        pltpu.make_async_remote_copy(
            send.at[pl.ds(at, CAP)], recv.at[pl.ds(at, CAP)], ss.at[0], rs.at[(a * ys + c) // per],
            device_id=(band, there), device_id_type=MESH,
        ).start()
    for k in range(1, bands):
        pltpu.make_async_remote_copy(
            meta_out, meta_in.at[k], ms.at[0], mr.at[0],
            device_id=((band + k) % bands, dom), device_id_type=MESH,
        ).start()
    recv[pl.ds(0, CAP), :] = send[pl.ds(0, CAP), :]

    sender = enc_s[...]
    from_dom = sender // CAP
    rel_z = (z - from_dom // ys + zs) % zs
    rel_y = (y - from_dom % ys + ys) % ys
    place = lanes_to_rows((rel_z * ys + rel_y) * CAP + sender % CAP)
    for i in range(slots // 128):
        pick[:, pl.ds(i * 128, 128)] = one_hot(place == iota((edges, 128), 1) + i * 128)
    lane = iota((edges, 128), 1)
    receiver = lanes_to_rows(enc_r[...])
    recv_hot = one_hot(((lane % count) == receiver) & (lane < 2 * count))
    hot_t = one_hot(iota((count, edges), 0) == enc_r[...])
    for load in loads[9:]:
        load.wait()
    recv_proj = dot(rows[...], e_w1[width:]) + e_b1[...]
    stack = jnp.concatenate([halves(recv_proj), jnp.zeros((128 - 2 * count, recv_proj.shape[1]), BF16)], axis=0)
    base[...] = dot(recv_hot, stack)
    node_pre = dot(rows[...], n_w1[:width]) + en_b1[...]
    proc_send, proc_recv = lanes_to_rows(proc_s[...]), lanes_to_rows(proc_r[...])
    proc_hot = one_hot((lane % count) == jnp.where((lane // count) % 2 == 0, proc_send, proc_recv))
    proc_hot_t = one_hot(iota((count, edges), 0) == proc_r[...])
    pack = one_hot(packs)
    stays = one_hot(dest - band * count == iota((count, count), 0))
    pltpu.make_async_remote_copy(
        meta_in.at[pl.ds(1, bands - 1)], meta_in.at[pl.ds(1, bands - 1)], ms.at[0], mr.at[0],
        device_id=((band + 1) % bands, dom), device_id_type=MESH,
    ).wait()
    moved = meta_in[...].reshape(bands * 2 * MOVE, 128)
    moved = jnp.concatenate([moved[i * 128 : (i + 1) * 128].T for i in range(bands * 2 * MOVE // 128)], axis=1)
    lands = moved[:count] == iota((count, bands * 2 * MOVE), 0) + band * count
    left = (iota((count, bands * 2 * MOVE), 1) % (2 * MOVE)) < MOVE
    place_in = jnp.concatenate([one_hot(lands & left), one_hot(lands & jnp.logical_not(left))], axis=0)

    span = per * CAP
    for i in range(chunks):
        first = 1 if i == 0 else i * per
        blocks = per - 1 if i == 0 else per
        landed = recv.at[pl.ds(first * CAP, blocks * CAP)]
        pltpu.make_async_remote_copy(
            landed, landed, ss.at[0], rs.at[i], device_id=(band, (z * ys + (y + 1) % ys)), device_id_type=MESH
        ).wait_recv()
        part = dot(pick[:, pl.ds(i * span, span)], recv[pl.ds(i * span, span), :])
        if i == 0:
            total[...] = part
        elif i < chunks - 1:
            total[...] += part
    gathered = (total[...] + part).astype(BF16) if chunks > 1 else part.astype(BF16)
    hidden = silu(base[...] + dot(gathered, e_w1[:width])).astype(BF16)
    agg = aggregate(hidden, hot_t, e_w2, e_b2[...])
    mesh_enc = node_out(rows[...], node_pre, agg, n_w1, n_w2, en_b2[...], e_gain[...])

    packed = dot(pack, mesh_enc)
    move_out[...] = jnp.concatenate([packed[:, : width // 2], packed[:, width // 2 :]], axis=0).astype(BF16)
    for k in range(1, bands):
        pltpu.make_async_remote_copy(
            move_out, move_in.at[k], vs.at[0], vr.at[0],
            device_id=((band + k) % bands, dom), device_id_type=MESH,
        ).start()
    kept = dot(stays, mesh_enc)
    pltpu.make_async_remote_copy(
        move_in.at[pl.ds(1, bands - 1)], move_in.at[pl.ds(1, bands - 1)], vs.at[0], vr.at[0],
        device_id=((band + 1) % bands, dom), device_id_type=MESH,
    ).wait()
    came = dot(place_in, move_in[...].reshape(bands * 2 * MOVE, width // 2))
    proc_in = (kept + jnp.concatenate([came[:count], came[count:]], axis=1)).astype(BF16)

    projected = jnp.concatenate([dot(proc_in, p_w1[:width]), dot(proc_in, p_w1[width:]) + p_b1[...]], axis=0)
    hidden = silu(dot(proc_hot, halves(projected))).astype(BF16)
    node_pre = dot(proc_in, q_w1[:width]) + pn_b1[...]
    agg = aggregate(hidden, proc_hot_t, p_w2, p_b2[...])
    out[...] = node_out(proc_in, node_pre, agg, q_w1, q_w2, pn_b2[...], p_gain[...])
    outgoing = send.at[pl.ds(CAP, slots - CAP)]
    pltpu.make_async_remote_copy(
        outgoing, outgoing, ss.at[0], rs.at[0], device_id=(band, (z * ys + (y + 1) % ys)), device_id_type=MESH
    ).wait_send()


def solution(mesh):
    bands, doms = mesh.shape["band"], mesh.shape["dom"]
    zs = 2 ** ((doms.bit_length() - 1) // 2)
    ys = doms // zs
    offsets = [(a, c) for a in range(zs) for c in range(ys) if (a, c) != (0, 0)]
    order = [offsets[i] for i in np.random.RandomState(0).permutation(len(offsets))]

    def shards(
        grid_latent, mesh_latent, send_rows, send_count, enc_sender, enc_receiver, move_to, proc_sender, proc_receiver,
        enc_edge_w1, enc_edge_b1, enc_edge_w2, enc_edge_b2, enc_node_w1, enc_node_b1, enc_node_w2, enc_node_b2, enc_gain,
        proc_edge_w1, proc_edge_b1, proc_edge_w2, proc_edge_b2, proc_node_w1, proc_node_b1, proc_node_w2, proc_node_b2, proc_gain,
    ):
        count, width = mesh_latent.shape
        edges = enc_sender.shape[0]
        slots = doms * CAP
        row = lambda a: a.reshape(1, -1)
        operands = (
            send_rows.T, row(send_count), grid_latent, row(move_to), row(enc_sender), mesh_latent, row(enc_receiver),
            row(proc_sender), row(proc_receiver),
            enc_edge_w1, row(enc_edge_b1), enc_node_w1, row(enc_node_b1), enc_edge_w2, row(enc_edge_b2),
            enc_node_w2, row(enc_node_b2), row(enc_gain),
            proc_edge_w1, row(proc_edge_b1), proc_edge_w2, row(proc_edge_b2), proc_node_w1, row(proc_node_b1),
            proc_node_w2, row(proc_node_b2), row(proc_gain),
        )
        vmem = pl.BlockSpec(memory_space=pltpu.VMEM)
        dma = pltpu.SemaphoreType.DMA
        chunks = max(1, slots // 256)
        return pl.pallas_call(
            functools.partial(kernel, bands, zs, ys, order),
            out_shape=jax.ShapeDtypeStruct((count, width), BF16),
            in_specs=[pl.BlockSpec(memory_space=pltpu.HBM)] * ARGS,
            out_specs=vmem,
            scratch_shapes=[pltpu.VMEM(w.shape, w.dtype) for w in operands] + [
                pltpu.VMEM((slots, width), BF16),
                pltpu.VMEM((slots, width), BF16),
                pltpu.VMEM((edges, slots), BF16),
                pltpu.VMEM((edges, enc_edge_w1.shape[1]), F32),
                pltpu.VMEM((edges, width), F32),
                pltpu.VMEM((2 * MOVE, 128), I32),
                pltpu.VMEM((bands, 2 * MOVE, 128), I32),
                pltpu.VMEM((2 * MOVE, width // 2), BF16),
                pltpu.VMEM((bands, 2 * MOVE, width // 2), BF16),
                dma((ARGS,)), dma((1,)), dma((chunks,)), dma((1,)), dma((1,)), dma((1,)), dma((1,)),
            ],
            compiler_params=pltpu.CompilerParams(
                collective_id=0, has_side_effects=True, vmem_limit_bytes=63 * 1024 * 1024
            ),
            name="encode_process",
        )(*operands)

    split, whole = P(("band", "dom")), P()
    return jax.shard_map(
        shards,
        mesh=mesh,
        in_specs=(P(("band", "dom"), None),) * 3 + (split,) * 6 + (whole,) * 18,
        out_specs=P(("band", "dom"), None),
        check_vma=False,
    )
```

```python
import functools

import jax
import jax.numpy as jnp
import numpy as np
from jax import lax
from jax.experimental import pallas as pl
from jax.experimental.pallas import tpu as pltpu
from jax.sharding import PartitionSpec as P

MESH = pl.DeviceIdType.MESH
F32 = jnp.float32
BF16 = jnp.bfloat16
I32 = jnp.int32
CAP = 16
MOVE = 8
ARGS = 28


def iota(shape, dim):
    return lax.broadcasted_iota(I32, shape, dim)


def dot(a, b):
    return jnp.dot(a, b, preferred_element_type=F32)


def one_hot(mask):
    return jnp.where(mask, 1.0, 0.0).astype(BF16)


def silu(v):
    half = 0.5 * v
    return half + half * jnp.tanh(half)


def halves(v):
    high = v.astype(BF16)
    return jnp.concatenate([high, (v - high.astype(F32)).astype(BF16)], axis=0)


def node_out(rows, pre, agg, w1, w2, b2, gain):
    width = rows.shape[1]
    z = silu(pre + dot(agg, w1[width:])).astype(BF16)
    u = dot(z, w2[...]) + b2
    center = u - jnp.mean(u, axis=-1, keepdims=True)
    spread = jnp.mean(center * center, axis=-1, keepdims=True)
    return (rows.astype(F32) + gain * (center * lax.rsqrt(spread + 1e-05))).astype(BF16)


def aggregate(hidden, hot_t, w2, b2):
    rows = hot_t.shape[0]
    two = dot(halves(dot(hot_t, hidden)), w2[...])
    count = jnp.sum(hot_t.astype(F32), axis=1, keepdims=True)
    return (two[:rows] + two[rows:] + count * b2).astype(BF16)


def lanes_to_rows(row):
    return jnp.broadcast_to(row, (128, row.shape[1])).T


def far_order(zs, ys):
    hops = lambda v, n: min(v, n - v)
    far = lambda o: hops(o[0], zs) + hops(o[1], ys)
    opposite = lambda o: (-o[0] % zs, -o[1] % ys)
    order = []
    for o in sorted(((a, c) for a in range(zs) for c in range(ys)), key=far, reverse=True):
        swapped = (o[1] % zs, o[0] % ys)
        for q in (o, swapped, opposite(o), opposite(swapped)):
            if q not in order and q != (0, 0) and far(q) == far(o):
                order.append(q)
    return order


def kernel(
    bands, zs, ys, order,
    *refs,
):
    hbm, out = refs[:ARGS], refs[ARGS]
    held = refs[ARGS + 1 : 2 * ARGS + 1]
    (send, recv, pick, base, total, meta_out, meta_in, move_out, move_in,
     in_sem, ss, rs, ms, mr, vs, vr) = refs[2 * ARGS + 1 :]
    (send_rows, send_count, grid, turns, move_to, enc_s, rows, enc_r, proc_s, proc_r,
     e_w1, e_b1, n_w1, en_b1, e_w2, e_b2, n_w2, en_b2, e_gain,
     p_w1, p_b1, p_w2, p_b2, q_w1, pn_b1, q_w2, pn_b2, p_gain) = held
    doms = zs * ys
    width = grid.shape[1]
    count = rows.shape[0]
    edges = enc_s.shape[1]
    slots = doms * CAP
    chunks = rs.shape[0]
    per = doms // chunks
    band, dom = lax.axis_index("band"), lax.axis_index("dom")
    z, y = dom // ys, dom % ys

    sign = 1 - 2 * (band % 2)
    far_bands = sorted(range(1, bands), key=lambda k: -min(k, bands - k))

    def peer_at(a, c):
        return ((z + sign * a + zs) % zs) * ys + (y + sign * c + ys) % ys

    def turn(to_z, to_y):
        rel = ((sign * to_z) % zs) * ys + (sign * to_y) % ys
        hot = iota((doms, rel.shape[1]), 0) == rel
        return jnp.sum(jnp.where(hot, turns[:, :1], 0), axis=0, keepdims=True)

    loads = [pltpu.make_async_copy(hbm[i], held[i], in_sem.at[i]) for i in range(ARGS)]
    for load in loads[:4]:
        load.start()

    barrier = pltpu.get_barrier_semaphore()
    for a, c in order:
        pl.semaphore_signal(barrier, inc=1, device_id=(band, peer_at(a, c)), device_id_type=MESH)
    for k in far_bands:
        pl.semaphore_signal(barrier, inc=1, device_id=((band + k) % bands, dom), device_id_type=MESH)
    for load in loads[:4]:
        load.wait()

    span = per * CAP
    points = grid.shape[0]
    listed = send_rows[...].astype(F32).astype(BF16)
    counts = send_count[...].astype(F32)
    peers = iota((1, doms), 1)
    at_turn = turn(peers // ys - z, peers % ys - y)
    for i in range(chunks):
        peer = at_turn == iota((span, doms), 0) // CAP + i * per
        mine = lax.dot_general(one_hot(peer), listed, (((1,), (1,)), ((), ())), preferred_element_type=F32)
        lane = (iota((span, CAP), 0) % CAP) == iota((span, CAP), 1)
        index = dot(jnp.where(lane, mine, 0.0).astype(BF16), jnp.ones((CAP, points), BF16))
        limit = dot(jnp.where(peer, counts, 0.0).astype(BF16), jnp.ones((doms, points), BF16))
        at = iota((span, points), 0) % CAP
        hot = (index == iota((span, points), 1).astype(F32)) & (at.astype(F32) < limit)
        send[pl.ds(i * span, span), :] = dot(one_hot(hot), grid[...]).astype(BF16)
        if i == 0:
            pl.semaphore_wait(barrier, len(order) + bands - 1)
        for t in range(max(1, i * per), (i + 1) * per):
            pltpu.make_async_remote_copy(
                send.at[pl.ds(t * CAP, CAP)], recv.at[pl.ds(t * CAP, CAP)], ss.at[0], rs.at[i],
                device_id=(band, peer_at(*order[t - 1])), device_id_type=MESH,
            ).start()
    for load in loads[4:]:
        load.start()
    recv[pl.ds(0, CAP), :] = send[pl.ds(0, CAP), :]

    for load in loads[4:10]:
        load.wait()
    dest = move_to[...]
    leaves = (dest // count) != band
    before = one_hot(iota((count, count), 0) < iota((count, count), 1))
    rank = dot(jnp.broadcast_to(one_hot(leaves), (8, count)), before)[:MOVE]
    packs = (rank == iota((MOVE, count), 0).astype(F32)) & leaves
    goes = jnp.sum(jnp.where(packs, (dest + 1).astype(F32), 0.0), axis=1, keepdims=True) - 1.0
    goes = jnp.broadcast_to(goes, (MOVE, 128)).astype(I32)
    meta_out[...] = jnp.concatenate([goes, goes], axis=0)
    meta_in[0] = jnp.full((2 * MOVE, 128), -1, I32)
    move_in[0] = jnp.zeros((2 * MOVE, width // 2), BF16)
    for k in far_bands:
        pltpu.make_async_remote_copy(
            meta_out, meta_in.at[k], ms.at[0], mr.at[0],
            device_id=((band + k) % bands, dom), device_id_type=MESH,
        ).start()

    sender = enc_s[...]
    from_dom = sender // CAP
    place = lanes_to_rows(turn(z - from_dom // ys, y - from_dom % ys) * CAP + sender % CAP)
    for i in range(slots // 128):
        pick[:, pl.ds(i * 128, 128)] = one_hot(place == iota((edges, 128), 1) + i * 128)
    lane = iota((edges, 128), 1)
    receiver = lanes_to_rows(enc_r[...])
    recv_hot = one_hot(((lane % count) == receiver) & (lane < 2 * count))
    hot_t = one_hot(iota((count, edges), 0) == enc_r[...])
    for load in loads[10:]:
        load.wait()
    recv_proj = dot(rows[...], e_w1[width:]) + e_b1[...]
    stack = jnp.concatenate([halves(recv_proj), jnp.zeros((128 - 2 * count, recv_proj.shape[1]), BF16)], axis=0)
    base[...] = dot(recv_hot, stack)
    node_pre = dot(rows[...], n_w1[:width]) + en_b1[...]
    proc_send, proc_recv = lanes_to_rows(proc_s[...]), lanes_to_rows(proc_r[...])
    proc_hot = one_hot((lane % count) == jnp.where((lane // count) % 2 == 0, proc_send, proc_recv))
    proc_hot_t = one_hot(iota((count, edges), 0) == proc_r[...])
    pack = one_hot(packs)
    stays = one_hot(dest - band * count == iota((count, count), 0))
    pltpu.make_async_remote_copy(
        meta_in.at[pl.ds(1, bands - 1)], meta_in.at[pl.ds(1, bands - 1)], ms.at[0], mr.at[0],
        device_id=((band + 1) % bands, dom), device_id_type=MESH,
    ).wait()
    moved = meta_in[...].reshape(bands * 2 * MOVE, 128)
    moved = jnp.concatenate([moved[i * 128 : (i + 1) * 128].T for i in range(bands * 2 * MOVE // 128)], axis=1)
    lands = moved[:count] == iota((count, bands * 2 * MOVE), 0) + band * count
    left = (iota((count, bands * 2 * MOVE), 1) % (2 * MOVE)) < MOVE
    place_in = jnp.concatenate([one_hot(lands & left), one_hot(lands & jnp.logical_not(left))], axis=0)

    for i in range(chunks):
        first = 1 if i == 0 else i * per
        blocks = per - 1 if i == 0 else per
        landed = recv.at[pl.ds(first * CAP, blocks * CAP)]
        pltpu.make_async_remote_copy(
            landed, landed, ss.at[0], rs.at[i], device_id=(band, (z * ys + (y + 1) % ys)), device_id_type=MESH
        ).wait_recv()
        part = dot(pick[:, pl.ds(i * span, span)], recv[pl.ds(i * span, span), :])
        if i == 0:
            total[...] = part
        elif i < chunks - 1:
            total[...] += part
    gathered = (total[...] + part).astype(BF16) if chunks > 1 else part.astype(BF16)
    hidden = silu(base[...] + dot(gathered, e_w1[:width])).astype(BF16)
    agg = aggregate(hidden, hot_t, e_w2, e_b2[...])
    mesh_enc = node_out(rows[...], node_pre, agg, n_w1, n_w2, en_b2[...], e_gain[...])

    packed = dot(pack, mesh_enc)
    move_out[...] = jnp.concatenate([packed[:, : width // 2], packed[:, width // 2 :]], axis=0).astype(BF16)
    for k in far_bands:
        pltpu.make_async_remote_copy(
            move_out, move_in.at[k], vs.at[0], vr.at[0],
            device_id=((band + k) % bands, dom), device_id_type=MESH,
        ).start()
    kept = dot(stays, mesh_enc)
    pltpu.make_async_remote_copy(
        move_in.at[pl.ds(1, bands - 1)], move_in.at[pl.ds(1, bands - 1)], vs.at[0], vr.at[0],
        device_id=((band + 1) % bands, dom), device_id_type=MESH,
    ).wait()
    came = dot(place_in, move_in[...].reshape(bands * 2 * MOVE, width // 2))
    proc_in = (kept + jnp.concatenate([came[:count], came[count:]], axis=1)).astype(BF16)

    projected = jnp.concatenate([dot(proc_in, p_w1[:width]), dot(proc_in, p_w1[width:]) + p_b1[...]], axis=0)
    hidden = silu(dot(proc_hot, halves(projected))).astype(BF16)
    node_pre = dot(proc_in, q_w1[:width]) + pn_b1[...]
    agg = aggregate(hidden, proc_hot_t, p_w2, p_b2[...])
    out[...] = node_out(proc_in, node_pre, agg, q_w1, q_w2, pn_b2[...], p_gain[...])
    outgoing = send.at[pl.ds(CAP, slots - CAP)]
    pltpu.make_async_remote_copy(
        outgoing, outgoing, ss.at[0], rs.at[0], device_id=(band, (z * ys + (y + 1) % ys)), device_id_type=MESH
    ).wait_send()


def solution(mesh):
    bands, doms = mesh.shape["band"], mesh.shape["dom"]
    zs = 2 ** ((doms.bit_length() - 1) // 2)
    ys = doms // zs
    order = far_order(zs, ys)
    turns = np.zeros((doms, 128), np.int32)
    for t, (a, c) in enumerate(order):
        turns[a * ys + c] = t + 1

    def shards(
        grid_latent, mesh_latent, send_rows, send_count, enc_sender, enc_receiver, move_to, proc_sender, proc_receiver,
        enc_edge_w1, enc_edge_b1, enc_edge_w2, enc_edge_b2, enc_node_w1, enc_node_b1, enc_node_w2, enc_node_b2, enc_gain,
        proc_edge_w1, proc_edge_b1, proc_edge_w2, proc_edge_b2, proc_node_w1, proc_node_b1, proc_node_w2, proc_node_b2, proc_gain,
    ):
        count, width = mesh_latent.shape
        edges = enc_sender.shape[0]
        slots = doms * CAP
        row = lambda a: a.reshape(1, -1)
        operands = (
            send_rows.T, row(send_count), grid_latent, jnp.asarray(turns), row(move_to), row(enc_sender), mesh_latent, row(enc_receiver),
            row(proc_sender), row(proc_receiver),
            enc_edge_w1, row(enc_edge_b1), enc_node_w1, row(enc_node_b1), enc_edge_w2, row(enc_edge_b2),
            enc_node_w2, row(enc_node_b2), row(enc_gain),
            proc_edge_w1, row(proc_edge_b1), proc_edge_w2, row(proc_edge_b2), proc_node_w1, row(proc_node_b1),
            proc_node_w2, row(proc_node_b2), row(proc_gain),
        )
        vmem = pl.BlockSpec(memory_space=pltpu.VMEM)
        dma = pltpu.SemaphoreType.DMA
        chunks = max(1, slots // 256)
        return pl.pallas_call(
            functools.partial(kernel, bands, zs, ys, order),
            out_shape=jax.ShapeDtypeStruct((count, width), BF16),
            in_specs=[pl.BlockSpec(memory_space=pltpu.HBM)] * ARGS,
            out_specs=vmem,
            scratch_shapes=[pltpu.VMEM(w.shape, w.dtype) for w in operands] + [
                pltpu.VMEM((slots, width), BF16),
                pltpu.VMEM((slots, width), BF16),
                pltpu.VMEM((edges, slots), BF16),
                pltpu.VMEM((edges, enc_edge_w1.shape[1]), F32),
                pltpu.VMEM((edges, width), F32),
                pltpu.VMEM((2 * MOVE, 128), I32),
                pltpu.VMEM((bands, 2 * MOVE, 128), I32),
                pltpu.VMEM((2 * MOVE, width // 2), BF16),
                pltpu.VMEM((bands, 2 * MOVE, width // 2), BF16),
                dma((ARGS,)), dma((1,)), dma((chunks,)), dma((1,)), dma((1,)), dma((1,)), dma((1,)),
            ],
            compiler_params=pltpu.CompilerParams(
                collective_id=0, has_side_effects=True, vmem_limit_bytes=63 * 1024 * 1024
            ),
            name="encode_process",
        )(*operands)

    split, whole = P(("band", "dom")), P()
    return jax.shard_map(
        shards,
        mesh=mesh,
        in_specs=(P(("band", "dom"), None),) * 3 + (split,) * 6 + (whole,) * 18,
        out_specs=P(("band", "dom"), None),
        check_vma=False,
    )
```

```python
import functools

import jax
import jax.numpy as jnp
import numpy as np
from jax import lax
from jax.experimental import pallas as pl
from jax.experimental.pallas import tpu as pltpu
from jax.sharding import PartitionSpec as P

MESH = pl.DeviceIdType.MESH
F32 = jnp.float32
BF16 = jnp.bfloat16
I32 = jnp.int32
CAP = 16
MOVE = 8
ARGS = 28


def iota(shape, dim):
    return lax.broadcasted_iota(I32, shape, dim)


def dot(a, b):
    return jnp.dot(a, b, preferred_element_type=F32)


def one_hot(mask):
    return jnp.where(mask, 1.0, 0.0).astype(BF16)


def silu(v):
    half = 0.5 * v
    return half + half * jnp.tanh(half)


def halves(v):
    high = v.astype(BF16)
    return jnp.concatenate([high, (v - high.astype(F32)).astype(BF16)], axis=0)


def node_out(rows, pre, w2, b2, gain):
    z = silu(pre).astype(BF16)
    u = dot(z, w2[...]) + b2
    center = u - jnp.mean(u, axis=-1, keepdims=True)
    spread = jnp.mean(center * center, axis=-1, keepdims=True)
    return (rows.astype(F32) + gain * (center * lax.rsqrt(spread + 1e-05))).astype(BF16)


def fold(w2, b2, hot_t, w1, both):
    width, columns = w2.shape[1], w1.shape[1]
    product = dot(w2[...], w1[width:])
    high = product.astype(BF16)
    both[:, :columns] = high
    both[:, columns:] = (product - high.astype(F32)).astype(BF16)
    bias = dot(halves(jnp.broadcast_to(b2, (8, width))), w1[width:])
    count = jnp.sum(hot_t.astype(F32), axis=1, keepdims=True)
    return count * (bias[:1] + bias[8:9])


def edge_part(hidden_sum, both):
    rows, columns = hidden_sum.shape[0], both.shape[1] // 2
    two = dot(halves(hidden_sum), both[...])
    return two[:rows, :columns] + (two[rows:, :columns] + two[:rows, columns:])


def lanes_to_rows(row):
    return jnp.broadcast_to(row, (128, row.shape[1])).T


def far_order(zs, ys):
    hops = lambda v, n: min(v, n - v)
    far = lambda o: hops(o[0], zs) + hops(o[1], ys)
    opposite = lambda o: (-o[0] % zs, -o[1] % ys)
    order = []
    for o in sorted(((a, c) for a in range(zs) for c in range(ys)), key=lambda o: (-max(hops(o[0], zs), hops(o[1], ys)), -far(o))):
        swapped = (o[1] % zs, o[0] % ys)
        for q in (o, swapped, opposite(o), opposite(swapped)):
            if q not in order and q != (0, 0) and far(q) == far(o):
                order.append(q)
    return order


def kernel(
    bands, zs, ys, order,
    *refs,
):
    hbm, out = refs[:ARGS], refs[ARGS]
    held = refs[ARGS + 1 : 2 * ARGS + 1]
    (send, recv, pick, base, e_both, p_both, meta_out, meta_in, move_out, move_in,
     in_sem, ss, rs, ms, mr, vs, vr) = refs[2 * ARGS + 1 :]
    (send_rows, send_count, grid, turns, move_to, enc_s, rows, enc_r, proc_s, proc_r,
     e_w1, e_b1, n_w1, en_b1, e_w2, e_b2, n_w2, en_b2, e_gain,
     p_w1, p_b1, p_w2, p_b2, q_w1, pn_b1, q_w2, pn_b2, p_gain) = held
    doms = zs * ys
    width = grid.shape[1]
    count = rows.shape[0]
    edges = enc_s.shape[1]
    slots = doms * CAP
    chunks = rs.shape[0]
    per = doms // chunks
    band, dom = lax.axis_index("band"), lax.axis_index("dom")
    z, y = dom // ys, dom % ys

    sign = 1 - 2 * (band % 2)
    far_bands = sorted(range(1, bands), key=lambda k: -min(k, bands - k))

    def peer_at(a, c):
        return ((z + sign * a + zs) % zs) * ys + (y + sign * c + ys) % ys

    def turn(to_z, to_y):
        rel = ((sign * to_z) % zs) * ys + (sign * to_y) % ys
        hot = iota((doms, rel.shape[1]), 0) == rel
        return jnp.sum(jnp.where(hot, turns[:, :1], 0), axis=0, keepdims=True)

    loads = [pltpu.make_async_copy(hbm[i], held[i], in_sem.at[i]) for i in range(ARGS)]
    for load in loads[:4]:
        load.start()

    barrier = pltpu.get_barrier_semaphore()
    for a, c in order:
        pl.semaphore_signal(barrier, inc=1, device_id=(band, peer_at(a, c)), device_id_type=MESH)
    for k in far_bands:
        pl.semaphore_signal(barrier, inc=1, device_id=((band + k) % bands, dom), device_id_type=MESH)
    for load in loads[:4]:
        load.wait()

    span = per * CAP
    points = grid.shape[0]
    listed = send_rows[...].astype(F32).astype(BF16)
    counts = send_count[...].astype(F32)
    peers = iota((1, doms), 1)
    at_turn = turn(peers // ys - z, peers % ys - y)
    for i in range(chunks):
        peer = at_turn == iota((span, doms), 0) // CAP + i * per
        mine = lax.dot_general(one_hot(peer), listed, (((1,), (1,)), ((), ())), preferred_element_type=F32)
        lane = (iota((span, CAP), 0) % CAP) == iota((span, CAP), 1)
        index = dot(jnp.where(lane, mine, 0.0).astype(BF16), jnp.ones((CAP, points), BF16))
        limit = dot(jnp.where(peer, counts, 0.0).astype(BF16), jnp.ones((doms, points), BF16))
        at = iota((span, points), 0) % CAP
        hot = (index == iota((span, points), 1).astype(F32)) & (at.astype(F32) < limit)
        send[pl.ds(i * span, span), :] = dot(one_hot(hot), grid[...]).astype(BF16)
        if i == 0:
            pl.semaphore_wait(barrier, len(order) + bands - 1)
        for t in range(max(1, i * per), (i + 1) * per):
            pltpu.make_async_remote_copy(
                send.at[pl.ds(t * CAP, CAP)], recv.at[pl.ds(t * CAP, CAP)], ss.at[0], rs.at[i],
                device_id=(band, peer_at(*order[t - 1])), device_id_type=MESH,
            ).start()
    for load in loads[4:]:
        load.start()
    recv[pl.ds(0, CAP), :] = send[pl.ds(0, CAP), :]

    for load in loads[4:10]:
        load.wait()
    dest = move_to[...]
    leaves = (dest // count) != band
    before = one_hot(iota((count, count), 0) < iota((count, count), 1))
    rank = dot(jnp.broadcast_to(one_hot(leaves), (8, count)), before)[:MOVE]
    packs = (rank == iota((MOVE, count), 0).astype(F32)) & leaves
    goes = jnp.sum(jnp.where(packs, (dest + 1).astype(F32), 0.0), axis=1, keepdims=True) - 1.0
    goes = jnp.broadcast_to(goes, (MOVE, 128)).astype(I32)
    meta_out[...] = jnp.concatenate([goes, goes], axis=0)
    meta_in[0] = jnp.full((2 * MOVE, 128), -1, I32)
    move_in[0] = jnp.zeros((2 * MOVE, width // 2), BF16)
    for k in far_bands:
        pltpu.make_async_remote_copy(
            meta_out, meta_in.at[k], ms.at[0], mr.at[0],
            device_id=((band + k) % bands, dom), device_id_type=MESH,
        ).start()

    sender = enc_s[...]
    from_dom = sender // CAP
    place = lanes_to_rows(turn(z - from_dom // ys, y - from_dom % ys) * CAP + sender % CAP)
    for i in range(slots // 128):
        pick[:, pl.ds(i * 128, 128)] = one_hot(place == iota((edges, 128), 1) + i * 128)
    lane = iota((edges, 128), 1)
    receiver = lanes_to_rows(enc_r[...])
    recv_hot = one_hot(((lane % count) == receiver) & (lane < 2 * count))
    hot_t = one_hot(iota((count, edges), 0) == enc_r[...])
    for load in loads[10:]:
        load.wait()
    recv_proj = dot(rows[...], e_w1[width:]) + e_b1[...]
    stack = jnp.concatenate([halves(recv_proj), jnp.zeros((128 - 2 * count, recv_proj.shape[1]), BF16)], axis=0)
    base[...] = dot(recv_hot, stack)
    node_pre = dot(rows[...], n_w1[:width]) + en_b1[...] + fold(e_w2, e_b2[...], hot_t, n_w1, e_both)
    proc_send, proc_recv = lanes_to_rows(proc_s[...]), lanes_to_rows(proc_r[...])
    proc_hot = one_hot((lane % count) == jnp.where((lane // count) % 2 == 0, proc_send, proc_recv))
    proc_hot_t = one_hot(iota((count, edges), 0) == proc_r[...])
    proc_bias = fold(p_w2, p_b2[...], proc_hot_t, q_w1, p_both) + pn_b1[...]
    pack = one_hot(packs)
    stays = one_hot(dest - band * count == iota((count, count), 0))
    pltpu.make_async_remote_copy(
        meta_in.at[pl.ds(1, bands - 1)], meta_in.at[pl.ds(1, bands - 1)], ms.at[0], mr.at[0],
        device_id=((band + 1) % bands, dom), device_id_type=MESH,
    ).wait()
    moved = meta_in[...].reshape(bands * 2 * MOVE, 128)
    moved = jnp.concatenate([moved[i * 128 : (i + 1) * 128].T for i in range(bands * 2 * MOVE // 128)], axis=1)
    lands = moved[:count] == iota((count, bands * 2 * MOVE), 0) + band * count
    left = (iota((count, bands * 2 * MOVE), 1) % (2 * MOVE)) < MOVE
    place_in = jnp.concatenate([one_hot(lands & left), one_hot(lands & jnp.logical_not(left))], axis=0)

    for i in range(chunks):
        first = 1 if i == 0 else i * per
        blocks = per - 1 if i == 0 else per
        landed = recv.at[pl.ds(first * CAP, blocks * CAP)]
        pltpu.make_async_remote_copy(
            landed, landed, ss.at[0], rs.at[i], device_id=(band, (z * ys + (y + 1) % ys)), device_id_type=MESH
        ).wait_recv()
        parts = []
        for e in range(0, edges, 512):
            got = dot(pick[pl.ds(e, 512), pl.ds(i * span, span)], recv[pl.ds(i * span, span), :]).astype(BF16)
            pre = base[pl.ds(e, 512), :] + dot(got, e_w1[:width])
            if i < chunks - 1:
                base[pl.ds(e, 512), :] = pre
            else:
                parts.append(dot(hot_t[:, e : e + 512], silu(pre).astype(BF16)))
    mesh_enc = node_out(rows[...], node_pre + edge_part(sum(parts), e_both), n_w2, en_b2[...], e_gain[...])

    packed = dot(pack, mesh_enc)
    move_out[...] = jnp.concatenate([packed[:, : width // 2], packed[:, width // 2 :]], axis=0).astype(BF16)
    for k in far_bands:
        pltpu.make_async_remote_copy(
            move_out, move_in.at[k], vs.at[0], vr.at[0],
            device_id=((band + k) % bands, dom), device_id_type=MESH,
        ).start()
    kept = dot(stays, mesh_enc)
    pltpu.make_async_remote_copy(
        move_in.at[pl.ds(1, bands - 1)], move_in.at[pl.ds(1, bands - 1)], vs.at[0], vr.at[0],
        device_id=((band + 1) % bands, dom), device_id_type=MESH,
    ).wait()
    came = dot(place_in, move_in[...].reshape(bands * 2 * MOVE, width // 2))
    proc_in = (kept + jnp.concatenate([came[:count], came[count:]], axis=1)).astype(BF16)

    projected = jnp.concatenate([dot(proc_in, p_w1[:width]), dot(proc_in, p_w1[width:]) + p_b1[...]], axis=0)
    stack = halves(projected)
    node_pre = dot(proc_in, q_w1[:width]) + proc_bias
    parts = []
    for e in range(0, edges, 512):
        hidden = silu(dot(proc_hot[e : e + 512], stack)).astype(BF16)
        parts.append(dot(proc_hot_t[:, e : e + 512], hidden))
    out[...] = node_out(proc_in, node_pre + edge_part(sum(parts), p_both), q_w2, pn_b2[...], p_gain[...])
    outgoing = send.at[pl.ds(CAP, slots - CAP)]
    pltpu.make_async_remote_copy(
        outgoing, outgoing, ss.at[0], rs.at[0], device_id=(band, (z * ys + (y + 1) % ys)), device_id_type=MESH
    ).wait_send()


def solution(mesh):
    bands, doms = mesh.shape["band"], mesh.shape["dom"]
    zs = 2 ** ((doms.bit_length() - 1) // 2)
    ys = doms // zs
    order = far_order(zs, ys)
    turns = np.zeros((doms, 128), np.int32)
    for t, (a, c) in enumerate(order):
        turns[a * ys + c] = t + 1

    def shards(
        grid_latent, mesh_latent, send_rows, send_count, enc_sender, enc_receiver, move_to, proc_sender, proc_receiver,
        enc_edge_w1, enc_edge_b1, enc_edge_w2, enc_edge_b2, enc_node_w1, enc_node_b1, enc_node_w2, enc_node_b2, enc_gain,
        proc_edge_w1, proc_edge_b1, proc_edge_w2, proc_edge_b2, proc_node_w1, proc_node_b1, proc_node_w2, proc_node_b2, proc_gain,
    ):
        count, width = mesh_latent.shape
        edges = enc_sender.shape[0]
        slots = doms * CAP
        row = lambda a: a.reshape(1, -1)
        operands = (
            send_rows.T, row(send_count), grid_latent, jnp.asarray(turns), row(move_to), row(enc_sender), mesh_latent, row(enc_receiver),
            row(proc_sender), row(proc_receiver),
            enc_edge_w1, row(enc_edge_b1), enc_node_w1, row(enc_node_b1), enc_edge_w2, row(enc_edge_b2),
            enc_node_w2, row(enc_node_b2), row(enc_gain),
            proc_edge_w1, row(proc_edge_b1), proc_edge_w2, row(proc_edge_b2), proc_node_w1, row(proc_node_b1),
            proc_node_w2, row(proc_node_b2), row(proc_gain),
        )
        vmem = pl.BlockSpec(memory_space=pltpu.VMEM)
        dma = pltpu.SemaphoreType.DMA
        chunks = max(1, slots // 256)
        return pl.pallas_call(
            functools.partial(kernel, bands, zs, ys, order),
            out_shape=jax.ShapeDtypeStruct((count, width), BF16),
            in_specs=[pl.BlockSpec(memory_space=pltpu.HBM)] * ARGS,
            out_specs=vmem,
            scratch_shapes=[pltpu.VMEM(w.shape, w.dtype) for w in operands] + [
                pltpu.VMEM((slots, width), BF16),
                pltpu.VMEM((slots, width), BF16),
                pltpu.VMEM((edges, slots), BF16),
                pltpu.VMEM((edges, enc_edge_w1.shape[1]), F32),
                pltpu.VMEM((enc_edge_w2.shape[0], 2 * enc_node_w1.shape[1]), BF16),
                pltpu.VMEM((proc_edge_w2.shape[0], 2 * proc_node_w1.shape[1]), BF16),
                pltpu.VMEM((2 * MOVE, 128), I32),
                pltpu.VMEM((bands, 2 * MOVE, 128), I32),
                pltpu.VMEM((2 * MOVE, width // 2), BF16),
                pltpu.VMEM((bands, 2 * MOVE, width // 2), BF16),
                dma((ARGS,)), dma((1,)), dma((chunks,)), dma((1,)), dma((1,)), dma((1,)), dma((1,)),
            ],
            compiler_params=pltpu.CompilerParams(
                collective_id=0, has_side_effects=True, vmem_limit_bytes=63 * 1024 * 1024
            ),
            name="encode_process",
        )(*operands)

    split, whole = P(("band", "dom")), P()
    return jax.shard_map(
        shards,
        mesh=mesh,
        in_specs=(P(("band", "dom"), None),) * 3 + (split,) * 6 + (whole,) * 18,
        out_specs=P(("band", "dom"), None),
        check_vma=False,
    )
```

```python
import functools

import jax
import jax.numpy as jnp
import numpy as np
from jax import lax
from jax.experimental import pallas as pl
from jax.experimental.pallas import tpu as pltpu
from jax.sharding import PartitionSpec as P

MESH = pl.DeviceIdType.MESH
F32 = jnp.float32
BF16 = jnp.bfloat16
I32 = jnp.int32
CAP = 16
MOVE = 8
ARGS = 28


def iota(shape, dim):
    return lax.broadcasted_iota(I32, shape, dim)


def dot(a, b):
    return jnp.dot(a, b, preferred_element_type=F32)


def one_hot(mask):
    return jnp.where(mask, 1.0, 0.0).astype(BF16)


def silu(v):
    half = 0.5 * v
    return half + half * jnp.tanh(half)


def halves(v):
    high = v.astype(BF16)
    return jnp.concatenate([high, (v - high.astype(F32)).astype(BF16)], axis=0)


def node_out(rows, pre, w2, b2, gain):
    z = silu(pre).astype(BF16)
    u = dot(z, w2[...]) + b2
    center = u - jnp.mean(u, axis=-1, keepdims=True)
    spread = jnp.mean(center * center, axis=-1, keepdims=True)
    return (rows.astype(F32) + gain * (center * lax.rsqrt(spread + 1e-05))).astype(BF16)


def fold(w2, b2, hot_t, w1, both):
    width, columns = w2.shape[1], w1.shape[1]
    product = dot(w2[...], w1[width:])
    high = product.astype(BF16)
    both[:, :columns] = high
    both[:, columns:] = (product - high.astype(F32)).astype(BF16)
    bias = dot(halves(jnp.broadcast_to(b2, (8, width))), w1[width:])
    count = jnp.sum(hot_t.astype(F32), axis=1, keepdims=True)
    return count * (bias[:1] + bias[8:9])


def edge_part(hidden_sum, both):
    rows, columns = hidden_sum.shape[0], both.shape[1] // 2
    two = dot(halves(hidden_sum), both[...])
    return two[:rows, :columns] + (two[rows:, :columns] + two[:rows, columns:])


def lanes_to_rows(row):
    return jnp.broadcast_to(row, (128, row.shape[1])).T


def far_order(zs, ys):
    hops = lambda v, n: min(v, n - v)
    far = lambda o: hops(o[0], zs) + hops(o[1], ys)
    opposite = lambda o: (-o[0] % zs, -o[1] % ys)
    order = []
    for o in sorted(((a, c) for a in range(zs) for c in range(ys)), key=lambda o: (-max(hops(o[0], zs), hops(o[1], ys)), -far(o))):
        swapped = (o[1] % zs, o[0] % ys)
        for q in (o, swapped, opposite(o), opposite(swapped)):
            if q not in order and q != (0, 0) and far(q) == far(o):
                order.append(q)
    return order


def kernel(
    bands, zs, ys, order,
    *refs,
):
    hbm, out = refs[:ARGS], refs[ARGS]
    held = refs[ARGS + 1 : 2 * ARGS + 1]
    (send, recv, pick, base, e_both, p_both, meta_out, meta_in, move_out, move_in,
     in_sem, ss, rs, ms, mr, vs, vr) = refs[2 * ARGS + 1 :]
    (send_rows, send_count, grid, turns, move_to, enc_s, rows, enc_r, proc_s, proc_r,
     e_w1, e_b1, n_w1, en_b1, e_w2, e_b2, n_w2, en_b2, e_gain,
     p_w1, p_b1, p_w2, p_b2, q_w1, pn_b1, q_w2, pn_b2, p_gain) = held
    doms = zs * ys
    width = grid.shape[1]
    count = rows.shape[0]
    edges = enc_s.shape[1]
    slots = doms * CAP
    halves_in = rs.shape[0]
    group = doms // halves_in
    chunks = max(1, slots // 256)
    per = doms // chunks
    band, dom = lax.axis_index("band"), lax.axis_index("dom")
    z, y = dom // ys, dom % ys

    sign = 1 - 2 * (band % 2)
    far_bands = sorted(range(1, bands), key=lambda k: -min(k, bands - k))

    def peer_at(a, c):
        return ((z + sign * a + zs) % zs) * ys + (y + sign * c + ys) % ys

    def turn(to_z, to_y):
        rel = ((sign * to_z) % zs) * ys + (sign * to_y) % ys
        hot = iota((doms, rel.shape[1]), 0) == rel
        return jnp.sum(jnp.where(hot, turns[:, :1], 0), axis=0, keepdims=True)

    loads = [pltpu.make_async_copy(hbm[i], held[i], in_sem.at[i]) for i in range(ARGS)]
    for load in loads[:4]:
        load.start()

    barrier = pltpu.get_barrier_semaphore()
    for a, c in order:
        pl.semaphore_signal(barrier, inc=1, device_id=(band, peer_at(a, c)), device_id_type=MESH)
    for k in far_bands:
        pl.semaphore_signal(barrier, inc=1, device_id=((band + k) % bands, dom), device_id_type=MESH)
    for load in loads[:4]:
        load.wait()

    span = per * CAP
    points = grid.shape[0]
    listed = send_rows[...].astype(F32).astype(BF16)
    counts = send_count[...].astype(F32)
    peers = iota((1, doms), 1)
    at_turn = turn(peers // ys - z, peers % ys - y)
    for i in range(chunks):
        peer = at_turn == iota((span, doms), 0) // CAP + i * per
        mine = lax.dot_general(one_hot(peer), listed, (((1,), (1,)), ((), ())), preferred_element_type=F32)
        lane = (iota((span, CAP), 0) % CAP) == iota((span, CAP), 1)
        index = dot(jnp.where(lane, mine, 0.0).astype(BF16), jnp.ones((CAP, points), BF16))
        limit = dot(jnp.where(peer, counts, 0.0).astype(BF16), jnp.ones((doms, points), BF16))
        at = iota((span, points), 0) % CAP
        hot = (index == iota((span, points), 1).astype(F32)) & (at.astype(F32) < limit)
        send[pl.ds(i * span, span), :] = dot(one_hot(hot), grid[...]).astype(BF16)
        if i == 0:
            pl.semaphore_wait(barrier, len(order) + bands - 1)
        for t in range(max(1, i * per), (i + 1) * per):
            pltpu.make_async_remote_copy(
                send.at[pl.ds(t * CAP, CAP)], recv.at[pl.ds(t * CAP, CAP)], ss.at[0], rs.at[t // group],
                device_id=(band, peer_at(*order[t - 1])), device_id_type=MESH,
            ).start()
    for load in loads[4:]:
        load.start()
    recv[pl.ds(0, CAP), :] = send[pl.ds(0, CAP), :]

    for load in loads[4:10]:
        load.wait()
    dest = move_to[...]
    leaves = (dest // count) != band
    before = one_hot(iota((count, count), 0) < iota((count, count), 1))
    rank = dot(jnp.broadcast_to(one_hot(leaves), (8, count)), before)[:MOVE]
    packs = (rank == iota((MOVE, count), 0).astype(F32)) & leaves
    goes = jnp.sum(jnp.where(packs, (dest + 1).astype(F32), 0.0), axis=1, keepdims=True) - 1.0
    goes = jnp.broadcast_to(goes, (MOVE, 128)).astype(I32)
    meta_out[...] = jnp.concatenate([goes, goes], axis=0)
    meta_in[0] = jnp.full((2 * MOVE, 128), -1, I32)
    move_in[0] = jnp.zeros((2 * MOVE, width // 2), BF16)
    for k in far_bands:
        pltpu.make_async_remote_copy(
            meta_out, meta_in.at[k], ms.at[0], mr.at[0],
            device_id=((band + k) % bands, dom), device_id_type=MESH,
        ).start()

    sender = enc_s[...]
    from_dom = sender // CAP
    place = lanes_to_rows(turn(z - from_dom // ys, y - from_dom % ys) * CAP + sender % CAP)
    for i in range(slots // 128):
        pick[:, pl.ds(i * 128, 128)] = one_hot(place == iota((edges, 128), 1) + i * 128)
    lane = iota((edges, 128), 1)
    receiver = lanes_to_rows(enc_r[...])
    recv_hot = one_hot(((lane % count) == receiver) & (lane < 2 * count))
    hot_t = one_hot(iota((count, edges), 0) == enc_r[...])
    for load in loads[10:]:
        load.wait()
    recv_proj = dot(rows[...], e_w1[width:]) + e_b1[...]
    stack = jnp.concatenate([halves(recv_proj), jnp.zeros((128 - 2 * count, recv_proj.shape[1]), BF16)], axis=0)
    base[...] = dot(recv_hot, stack)
    node_pre = dot(rows[...], n_w1[:width]) + en_b1[...] + fold(e_w2, e_b2[...], hot_t, n_w1, e_both)
    proc_send, proc_recv = lanes_to_rows(proc_s[...]), lanes_to_rows(proc_r[...])
    proc_hot = one_hot((lane % count) == jnp.where((lane // count) % 2 == 0, proc_send, proc_recv))
    proc_hot_t = one_hot(iota((count, edges), 0) == proc_r[...])
    proc_bias = fold(p_w2, p_b2[...], proc_hot_t, q_w1, p_both) + pn_b1[...]
    pack = one_hot(packs)
    stays = one_hot(dest - band * count == iota((count, count), 0))
    pltpu.make_async_remote_copy(
        meta_in.at[pl.ds(1, bands - 1)], meta_in.at[pl.ds(1, bands - 1)], ms.at[0], mr.at[0],
        device_id=((band + 1) % bands, dom), device_id_type=MESH,
    ).wait()
    moved = meta_in[...].reshape(bands * 2 * MOVE, 128)
    moved = jnp.concatenate([moved[i * 128 : (i + 1) * 128].T for i in range(bands * 2 * MOVE // 128)], axis=1)
    lands = moved[:count] == iota((count, bands * 2 * MOVE), 0) + band * count
    left = (iota((count, bands * 2 * MOVE), 1) % (2 * MOVE)) < MOVE
    place_in = jnp.concatenate([one_hot(lands & left), one_hot(lands & jnp.logical_not(left))], axis=0)

    for i in range(halves_in):
        first = 1 if i == 0 else i * group
        blocks = group - 1 if i == 0 else group
        landed = recv.at[pl.ds(first * CAP, blocks * CAP)]
        pltpu.make_async_remote_copy(
            landed, landed, ss.at[0], rs.at[i], device_id=(band, (z * ys + (y + 1) % ys)), device_id_type=MESH
        ).wait_recv()
        parts = []
        for e in range(0, edges, 512):
            got = dot(pick[pl.ds(e, 512), pl.ds(i * group * CAP, group * CAP)], recv[pl.ds(i * group * CAP, group * CAP), :]).astype(BF16)
            pre = base[pl.ds(e, 512), :] + dot(got, e_w1[:width])
            if i < halves_in - 1:
                base[pl.ds(e, 512), :] = pre
            else:
                parts.append(dot(hot_t[:, e : e + 512], silu(pre).astype(BF16)))
    mesh_enc = node_out(rows[...], node_pre + edge_part(sum(parts), e_both), n_w2, en_b2[...], e_gain[...])

    packed = dot(pack, mesh_enc)
    move_out[...] = jnp.concatenate([packed[:, : width // 2], packed[:, width // 2 :]], axis=0).astype(BF16)
    for k in far_bands:
        pltpu.make_async_remote_copy(
            move_out, move_in.at[k], vs.at[0], vr.at[0],
            device_id=((band + k) % bands, dom), device_id_type=MESH,
        ).start()
    kept = dot(stays, mesh_enc)
    pltpu.make_async_remote_copy(
        move_in.at[pl.ds(1, bands - 1)], move_in.at[pl.ds(1, bands - 1)], vs.at[0], vr.at[0],
        device_id=((band + 1) % bands, dom), device_id_type=MESH,
    ).wait()
    came = dot(place_in, move_in[...].reshape(bands * 2 * MOVE, width // 2))
    proc_in = (kept + jnp.concatenate([came[:count], came[count:]], axis=1)).astype(BF16)

    projected = jnp.concatenate([dot(proc_in, p_w1[:width]), dot(proc_in, p_w1[width:]) + p_b1[...]], axis=0)
    stack = halves(projected)
    node_pre = dot(proc_in, q_w1[:width]) + proc_bias
    parts = []
    for e in range(0, edges, 512):
        hidden = silu(dot(proc_hot[e : e + 512], stack)).astype(BF16)
        parts.append(dot(proc_hot_t[:, e : e + 512], hidden))
    out[...] = node_out(proc_in, node_pre + edge_part(sum(parts), p_both), q_w2, pn_b2[...], p_gain[...])
    outgoing = send.at[pl.ds(CAP, slots - CAP)]
    pltpu.make_async_remote_copy(
        outgoing, outgoing, ss.at[0], rs.at[0], device_id=(band, (z * ys + (y + 1) % ys)), device_id_type=MESH
    ).wait_send()


def solution(mesh):
    bands, doms = mesh.shape["band"], mesh.shape["dom"]
    zs = 2 ** ((doms.bit_length() - 1) // 2)
    ys = doms // zs
    order = far_order(zs, ys)
    turns = np.zeros((doms, 128), np.int32)
    for t, (a, c) in enumerate(order):
        turns[a * ys + c] = t + 1

    def shards(
        grid_latent, mesh_latent, send_rows, send_count, enc_sender, enc_receiver, move_to, proc_sender, proc_receiver,
        enc_edge_w1, enc_edge_b1, enc_edge_w2, enc_edge_b2, enc_node_w1, enc_node_b1, enc_node_w2, enc_node_b2, enc_gain,
        proc_edge_w1, proc_edge_b1, proc_edge_w2, proc_edge_b2, proc_node_w1, proc_node_b1, proc_node_w2, proc_node_b2, proc_gain,
    ):
        count, width = mesh_latent.shape
        edges = enc_sender.shape[0]
        slots = doms * CAP
        row = lambda a: a.reshape(1, -1)
        operands = (
            send_rows.T, row(send_count), grid_latent, jnp.asarray(turns), row(move_to), row(enc_sender), mesh_latent, row(enc_receiver),
            row(proc_sender), row(proc_receiver),
            enc_edge_w1, row(enc_edge_b1), enc_node_w1, row(enc_node_b1), enc_edge_w2, row(enc_edge_b2),
            enc_node_w2, row(enc_node_b2), row(enc_gain),
            proc_edge_w1, row(proc_edge_b1), proc_edge_w2, row(proc_edge_b2), proc_node_w1, row(proc_node_b1),
            proc_node_w2, row(proc_node_b2), row(proc_gain),
        )
        vmem = pl.BlockSpec(memory_space=pltpu.VMEM)
        dma = pltpu.SemaphoreType.DMA
        return pl.pallas_call(
            functools.partial(kernel, bands, zs, ys, order),
            out_shape=jax.ShapeDtypeStruct((count, width), BF16),
            in_specs=[pl.BlockSpec(memory_space=pltpu.HBM)] * ARGS,
            out_specs=vmem,
            scratch_shapes=[pltpu.VMEM(w.shape, w.dtype) for w in operands] + [
                pltpu.VMEM((slots, width), BF16),
                pltpu.VMEM((slots, width), BF16),
                pltpu.VMEM((edges, slots), BF16),
                pltpu.VMEM((edges, enc_edge_w1.shape[1]), F32),
                pltpu.VMEM((enc_edge_w2.shape[0], 2 * enc_node_w1.shape[1]), BF16),
                pltpu.VMEM((proc_edge_w2.shape[0], 2 * proc_node_w1.shape[1]), BF16),
                pltpu.VMEM((2 * MOVE, 128), I32),
                pltpu.VMEM((bands, 2 * MOVE, 128), I32),
                pltpu.VMEM((2 * MOVE, width // 2), BF16),
                pltpu.VMEM((bands, 2 * MOVE, width // 2), BF16),
                dma((ARGS,)), dma((1,)), dma((2,)), dma((1,)), dma((1,)), dma((1,)), dma((1,)),
            ],
            compiler_params=pltpu.CompilerParams(
                collective_id=0, has_side_effects=True, vmem_limit_bytes=63 * 1024 * 1024
            ),
            name="encode_process",
        )(*operands)

    split, whole = P(("band", "dom")), P()
    return jax.shard_map(
        shards,
        mesh=mesh,
        in_specs=(P(("band", "dom"), None),) * 3 + (split,) * 6 + (whole,) * 18,
        out_specs=P(("band", "dom"), None),
        check_vma=False,
    )
```
